512 devices in a mesh: tensor: 8 (over y, core), prefix: 4 (over x), cont: 16 (over z).
Axes of the slice: x: 4, y: 4, z: 16, core: 2. Of those that a mesh axis runs over, the one named last changes fastest.
Arguments:
- states: bfloat16 [64, 128, 8192], P('cont', None, 'prefix'), may hold values from -12 to 12
- norm_gain: float32 [8192], P('prefix'), may hold values from 0.1 to 1.9
- query_weight: bfloat16 [8192, 8192], P(('prefix', 'cont'), 'tensor'), may hold values from -0.0625 to 0.0625
- key_weight: bfloat16 [8192, 1024], P(('prefix', 'cont'), 'tensor'), may hold values from -0.125 to 0.125
- value_weight: bfloat16 [8192, 1024], P(('prefix', 'cont'), 'tensor'), may hold values from -0.0625 to 0.0625
- prefix_keys: bfloat16 [4, 2048, 8, 128], P('prefix', 'cont', 'tensor'), may hold values from -160 to 160
- prefix_values: bfloat16 [4, 2048, 8, 128], P('prefix', 'cont', 'tensor'), may hold values from -6 to 6
- path_prefix: int32 [64], P('cont'), may hold values from 0 to 3
- out_weight: bfloat16 [8192, 8192], P('tensor', ('prefix', 'cont')), may hold values from -0.0625 to 0.0625
- final_gain: float32 [4, 2048], P('prefix', 'tensor'), may hold values from 0.1 to 1.9
- head_weight: bfloat16 [4, 2048, 8192], P('prefix', 'tensor', 'cont'), may hold values from -3 to 3
- targets: int32 [64, 8], P(('tensor', 'prefix')), may hold values from 0 to 8191
- questions: int32 [64, 1], replicated, may hold values from 0 to 7
Outputs:
- context: bfloat16 [16, 4, 128, 8192], P('cont', 'prefix', None, 'tensor')
- scored_hidden: bfloat16 [64, 8, 4, 2048], P('cont', None, 'prefix', 'tensor')
- token_logprob: float32 [64, 8], P(('tensor', 'prefix'))
- path_score: float32 [64], P(('tensor', 'prefix'))
- question_score: float32 [8], replicated
The draws below stay inside these ranges and needn't reach their ends.
Inputs may be any that keep to these rules, and one draw needn't show every extreme that they name: Every one of the 8 questions has at least one path.
All inputs are finite; a program needn't handle non-finite values.
Results may differ from the reference program's by a relative error of at most 0.018.
The reference program's roundings to bfloat16 on the way (of `normed`, `weights` and `final_normed`) count: a program that leaves them out, or rounds other values in their place, can miss the bound.
Values may be sent and summed in bfloat16 or wider, within the bound.
No kernel may reach another device: no remote copies, remote signals or barrier semaphores. Data moves between devices by JAX's collectives and lax.ppermute only.
A program may use at most 128 MiB of HBM per device.

```python
import math
import jax
import jax.numpy as jnp
import numpy as np
from jax import lax

D = 8192
KVH = 8
HD = 128
QH = 64
VOCAB = 8192
CLEN = 128
SCORED = 8
PATH_DEV = 4
QUESTIONS = 8
PREFIXES = 4
PLEN = 2048
PATHS = 64
N_CONT = 16


def feature_ramp(low, ratio):
    place = jnp.arange(D, dtype=jnp.float32) / (D - 1)
    return low * jnp.exp(math.log(ratio) * place)


def draw_states(key, part):
    key = jax.random.fold_in(key, 3)
    noise_key = jax.random.fold_in(key, 0)
    extent = (PATHS, CLEN, D)
    ramp = feature_ramp(0.1, 30.0)
    return (jax.random.truncated_normal(noise_key, -4.0, 4.0, extent, jnp.float32) * ramp).astype(jnp.bfloat16)


def draw_prefix_keys(key, part):
    key = jax.random.fold_in(key, 11)
    base_key = jax.random.fold_in(key, 0)
    extent = (PREFIXES, PLEN, KVH, HD)
    return (2.0 * jax.random.truncated_normal(base_key, -6.0, 6.0, extent, jnp.float32)).astype(jnp.bfloat16)


def draw_head_weight(key, part):
    key = jax.random.fold_in(key, 17)
    base_key = jax.random.fold_in(key, 0)
    extent = (PREFIXES, D // PREFIXES, VOCAB)
    spread = 3.0 / math.sqrt(D)
    return (spread * jax.random.truncated_normal(base_key, -6.0, 6.0, extent, jnp.float32)).astype(jnp.bfloat16)


def with_ends(values, stream_key, smallest, largest):
    index_at = [jax.random.randint(jax.random.fold_in(stream_key, axis), (), 0, length) for axis, length in enumerate(values.shape)]
    main_axis = values.shape.index(max(values.shape))
    next_to = index_at[:main_axis] + [(index_at[main_axis] + 1) % values.shape[main_axis]] + index_at[main_axis + 1:]
    return values.at[tuple(index_at)].set(smallest).at[tuple(next_to)].set(largest)


def steps_of(stream_key, shape, pieces, smallest, high):
    gain = 1.0
    for position, blocks in pieces:
        draws = jax.random.uniform(jax.random.fold_in(jax.random.fold_in(stream_key, 6), position), (blocks,), jnp.float32, smallest / len(pieces), high / len(pieces))
        gain = gain * jnp.repeat(jnp.exp(draws), shape[position] // blocks).reshape((-1,) + (1,) * (len(shape) - 1 - position))
    return gain


def rank_table(count, lean):
    weights = [(1 << 20) // math.isqrt(rank ** lean) + 1 for rank in range(1, count + 1)]
    scale = 1 + sum(weights) // (1 << 30)
    return np.cumsum(np.array([max(1, weight // scale) for weight in weights]))


def ranked(key, dims, number_of, skew):
    listing = rank_table(number_of, skew)
    ticket = jax.random.randint(jax.random.fold_in(key, 1), dims, 0, int(listing[number_of - 1]))
    rank = jnp.searchsorted(jnp.asarray(listing, jnp.int32), ticket, side="right")
    return jax.random.permutation(jax.random.fold_in(key, 2), number_of)[rank].astype(jnp.int32)


def choose_distinct(key, rows, amount, top, lift):
    order = jax.random.permutation(jax.random.fold_in(key, 1), amount)
    pull = order
    for power in range(3):
        pull = pull * pull // amount
    pull = pull * lift // amount
    chance = jax.random.randint(jax.random.fold_in(key, 2), (rows, amount), 0, 4096) + pull
    holders = jax.random.permutation(jax.random.fold_in(key, 3), rows)[jnp.arange(amount) % rows]
    chance = jnp.where(jnp.arange(rows)[:, None] == holders[None, :], 1 << 14, chance)
    score = chance * amount + jnp.arange(amount)
    return lax.top_k(score.astype(jnp.int32), top)[1].astype(jnp.int32)


def centred(key, shape, deviation, reach, cuts=(), held_as=jnp.bfloat16):
    drawn = deviation * jax.random.normal(key, shape, jnp.float32)
    if cuts:
        drawn = drawn * steps_of(key, shape, cuts, -0.22, 0.18)
    return jnp.clip(drawn, -reach, reach).astype(held_as)


def setup_inputs(seed: int = 0) -> dict:
    streams_of = jax.random.split(jax.random.key(seed), 14)
    states = draw_states(jax.random.fold_in(streams_of[13], 71), 0)
    norm_gain = jnp.clip(1.0 + 0.18 * jax.random.normal(streams_of[1], (D,), jnp.float32), 0.1, 1.9)
    query_weight = centred(streams_of[2], (D, QH * HD), D ** -0.5, 0.0625, ((0, 64), (1, 8)))
    key_weight = centred(streams_of[3], (D, KVH * HD), (D // 4) ** -0.5, 0.125, ((0, 64), (1, 8)))
    value_weight = centred(streams_of[4], (D, KVH * HD), D ** -0.5, 0.0625, ((0, 64), (1, 8)))
    prefix_keys = draw_prefix_keys(jax.random.fold_in(streams_of[13], 71), 0)
    prefix_values = centred(streams_of[6], (PREFIXES, PLEN, KVH, HD), 1.0, 6.0, ((0, 4), (1, 16), (2, 8)))
    path_prefix = with_ends(ranked(streams_of[7], (PATHS,), PREFIXES, 2), jax.random.fold_in(streams_of[7], 3), 0, PREFIXES - 1).astype(jnp.int32)
    out_weight = centred(streams_of[8], (QH * HD, D), (QH * HD) ** -0.5, 0.0625, ((0, 8), (1, 64)))
    final_gain = jnp.clip(1.0 + 0.18 * jax.random.normal(streams_of[9], (PREFIXES, D // PREFIXES), jnp.float32), 0.1, 1.9)
    head_weight = draw_head_weight(jax.random.fold_in(streams_of[13], 71), 0)
    targets = with_ends(jax.random.randint(streams_of[11], (PATHS, SCORED), 0, VOCAB), jax.random.fold_in(streams_of[11], 1), 0, VOCAB - 1).astype(jnp.int32)
    questions = choose_distinct(streams_of[12], PATHS, QUESTIONS, 1, 1024)
    return dict(states=states, norm_gain=norm_gain, query_weight=query_weight, key_weight=key_weight, value_weight=value_weight, prefix_keys=prefix_keys, prefix_values=prefix_values, path_prefix=path_prefix, out_weight=out_weight, final_gain=final_gain, head_weight=head_weight, targets=targets, questions=questions)


epsilon = 1e-05
rope_base = 500000.0

def rotate(vectors, positions):
    half_dim = vectors.shape[-1] // 2
    ladder = jnp.arange(half_dim, dtype=jnp.float32) * (2.0 / vectors.shape[-1])
    inverse = jnp.exp(-math.log(rope_base) * ladder)
    angles = positions.astype(jnp.float32)[:, None] * inverse[None, :]
    cosine = jnp.cos(angles)[:, None, :]
    sine_part = jnp.sin(angles)[:, None, :]
    first_half = vectors[..., :half_dim]
    second_half = vectors[..., half_dim:]
    return jnp.concatenate([first_half * cosine - second_half * sine_part, second_half * cosine + first_half * sine_part], axis=-1)

def reference(states, norm_gain, query_weight, key_weight, value_weight, prefix_keys, prefix_values, path_prefix, out_weight, final_gain, head_weight, targets, questions):
    inputs = states.astype(jnp.float32)
    scaling = lax.rsqrt(lax.optimization_barrier(jnp.mean(inputs * inputs, axis=-1, keepdims=True)) + epsilon)
    normed = (inputs * scaling * norm_gain).astype(jnp.bfloat16).reshape(PATHS * CLEN, D)
    positions = PLEN + jnp.arange(CLEN, dtype=jnp.int32)
    queries = jnp.dot(normed, query_weight, preferred_element_type=jnp.float32).reshape(PATHS, CLEN, QH, HD)
    fresh_keys = jnp.dot(normed, key_weight, preferred_element_type=jnp.float32).reshape(PATHS, CLEN, KVH, HD)
    fresh_values = jnp.dot(normed, value_weight, preferred_element_type=jnp.float32).reshape(PATHS, CLEN, KVH, HD)
    queries = rotate(queries, positions).astype(jnp.bfloat16)
    fresh_keys = rotate(fresh_keys, positions).astype(jnp.bfloat16)
    fresh_values = fresh_values.astype(jnp.bfloat16)
    group_size = QH // KVH
    key_index = jnp.arange(PLEN + CLEN, dtype=jnp.int32)
    query_index = jnp.arange(CLEN, dtype=jnp.int32)
    allowed = (key_index[None, :] < PLEN) | (key_index[None, :] - PLEN <= query_index[:, None])

    def attend(operands):
        query_block, key_block, value_block, owner_index = operands
        cached_keys = lax.dynamic_index_in_dim(prefix_keys, owner_index, 0, keepdims=False)
        cached_values = lax.dynamic_index_in_dim(prefix_values, owner_index, 0, keepdims=False)
        every_key = jnp.concatenate([cached_keys, key_block], axis=0).astype(jnp.float32)
        every_value = jnp.concatenate([cached_values, value_block], axis=0).astype(jnp.float32)
        grouped = query_block.reshape(CLEN, KVH, group_size, HD).astype(jnp.float32)
        scores = jnp.einsum('qkgd,nkd->kgqn', grouped, every_key) * (1.0 / math.sqrt(HD))
        scores = jnp.where(allowed[None, None], scores, -jnp.inf)
        highest = lax.optimization_barrier(jnp.max(scores, axis=-1, keepdims=True))
        raised = jnp.exp(scores - highest)
        weights = lax.optimization_barrier(raised.astype(jnp.bfloat16)).astype(jnp.float32)
        totals = lax.optimization_barrier(jnp.sum(raised, axis=-1)).transpose(2, 0, 1)
        blended = jnp.einsum('kgqn,nkd->qkgd', weights, every_value) / totals[..., None]
        return blended.reshape(CLEN, QH * HD).astype(jnp.bfloat16)
    context = lax.map(attend, (queries, fresh_keys, fresh_values, path_prefix))
    scored_context = context[:, CLEN - SCORED:, :].reshape(PATHS * SCORED, QH * HD)
    projected = jnp.dot(scored_context, out_weight, preferred_element_type=jnp.float32)
    residual = states[:, CLEN - SCORED:, :].reshape(PATHS * SCORED, D).astype(jnp.float32)
    hidden = (projected + residual).astype(jnp.bfloat16)
    widened = hidden.astype(jnp.float32)
    final_scale = lax.rsqrt(lax.optimization_barrier(jnp.mean(widened * widened, axis=-1, keepdims=True)) + epsilon)
    final_normed = (widened * final_scale * final_gain.reshape(D)).astype(jnp.bfloat16)
    logits = jnp.dot(final_normed, head_weight.reshape(D, VOCAB), preferred_element_type=jnp.float32)
    highest_logit = lax.optimization_barrier(jnp.max(logits, axis=-1))
    log_total = highest_logit + jnp.log(lax.optimization_barrier(jnp.sum(jnp.exp(logits - highest_logit[:, None]), axis=-1)))
    picked = jnp.take_along_axis(logits, targets.reshape(PATHS * SCORED, 1), axis=1)[:, 0]
    token_logprob = (picked - log_total).reshape(PATHS, SCORED)
    path_score = lax.optimization_barrier(jnp.mean(token_logprob, axis=-1))
    labels = jnp.arange(QUESTIONS, dtype=jnp.int32)
    member = (questions[:, 0][:, None] == labels[None, :]).astype(jnp.float32)
    question_score = lax.optimization_barrier(jnp.sum(member * path_score[:, None], axis=0)) / lax.optimization_barrier(jnp.sum(member, axis=0))
    return (context.reshape(N_CONT, PATH_DEV, CLEN, QH * HD), hidden.reshape(PATHS, SCORED, PREFIXES, D // PREFIXES), token_logprob, path_score, question_score)
```

```python
import math

import jax
import jax.numpy as jnp
from jax import lax
from jax.experimental import pallas as pl
from jax.experimental.pallas import tpu as pltpu
from jax.sharding import PartitionSpec as P

SCORED = 8
QUESTIONS = 8
RESIDUES = 2

epsilon = 1e-05
rope_base = 500000.0
far_below = -1e30


def rope_tables(head_width, positions):
    half_dim = head_width // 2
    ladder = jnp.arange(half_dim, dtype=jnp.float32) * (2.0 / head_width)
    inverse = jnp.exp(-math.log(rope_base) * ladder)
    angles = positions.astype(jnp.float32)[:, None] * inverse[None, :]
    cosine, sine = jnp.cos(angles), jnp.sin(angles)
    return jnp.concatenate([cosine, cosine], -1), jnp.concatenate([-sine, sine], -1)


def rotate(vectors, cosine, sine):
    half = vectors.shape[-1] // 2
    swapped = jnp.concatenate([vectors[..., half:], vectors[..., :half]], -1)
    return vectors * cosine + swapped * sine


def attend_kernel(q_ref, cos_ref, sin_ref, kf_ref, vf_ref, kp_ref, vp_ref, out_ref):
    length, width = cos_ref.shape
    heads = q_ref.shape[1] // width
    cosine, sine = cos_ref[...], sin_ref[...]
    turned = []
    for h in range(heads):
        q = q_ref[:, h * width : (h + 1) * width]
        turned.append((q * cosine + pltpu.roll(q, width // 2, 1) * sine).astype(jnp.bfloat16))
    queries = jnp.concatenate(turned, 0)
    contract = (((1,), (1,)), ((), ()))
    old = lax.dot_general(queries, kp_ref[...], contract, preferred_element_type=jnp.float32)
    new = lax.dot_general(queries, kf_ref[...], contract, preferred_element_type=jnp.float32)
    row = lax.broadcasted_iota(jnp.int32, (length, length), 0)
    column = lax.broadcasted_iota(jnp.int32, (length, length), 1)
    allowed = jnp.concatenate([column <= row] * heads, 0)
    new = jnp.where(allowed, new, far_below)
    peak = jnp.maximum(jnp.max(old, -1, keepdims=True), jnp.max(new, -1, keepdims=True))
    factor = math.log2(math.e) / math.sqrt(width)
    old = jnp.exp2((old - peak) * factor)
    new = jnp.exp2((new - peak) * factor)
    total = jnp.sum(old, -1, keepdims=True) + jnp.sum(new, -1, keepdims=True)
    mixed = jnp.dot(old.astype(jnp.bfloat16), vp_ref[...], preferred_element_type=jnp.float32)
    mixed += jnp.dot(new.astype(jnp.bfloat16), vf_ref[...], preferred_element_type=jnp.float32)
    mixed = (mixed / total).astype(jnp.bfloat16)
    for h in range(heads):
        out_ref[:, h * width : (h + 1) * width] = mixed[h * length : (h + 1) * length]


def attend(q, cosine, sine, fresh_keys, fresh_values, keys, values):
    length, columns = q.shape
    width = cosine.shape[1]
    pair = 2 * width
    whole = lambda array: pl.BlockSpec(array.shape, lambda i: (0, 0))
    count = (columns // width) * length * (keys.shape[0] + length)
    return pl.pallas_call(
        attend_kernel,
        grid=(columns // pair,),
        in_specs=[
            pl.BlockSpec((length, pair), lambda i: (0, i)),
            whole(cosine),
            whole(sine),
            whole(fresh_keys),
            whole(fresh_values),
            whole(keys),
            whole(values),
        ],
        out_specs=pl.BlockSpec((length, pair), lambda i: (0, i)),
        out_shape=jax.ShapeDtypeStruct((length, columns), jnp.bfloat16),
        compiler_params=pltpu.CompilerParams(vmem_limit_bytes=40 * 1024 * 1024),
        cost_estimate=pl.CostEstimate(
            flops=4 * count * width, bytes_accessed=2 * 1024 * 1024, transcendentals=count
        ),
    )(q, cosine, sine, fresh_keys, fresh_values, keys, values)


def output_kernel(rows_ref, weight_ref, out_ref):
    pieces, cont_rows, _ = out_ref.shape
    blocks, _, width = weight_ref.shape
    spans = blocks // 2
    rows = rows_ref[...]
    for j in range(blocks):
        product = jnp.dot(rows, weight_ref[j], preferred_element_type=jnp.float32)
        for k in range(pieces // spans):
            out_ref[k * spans + j // 2, :, (j % 2) * width : (j % 2 + 1) * width] = product[
                k * cont_rows : (k + 1) * cont_rows
            ]


def after(array, earlier):
    return lax.optimization_barrier((array, earlier))[0]


def everyone(array, axis, groups=None):
    size = len(groups[0]) if groups else lax.axis_size(axis)
    spread = jnp.broadcast_to(array[None], (size,) + array.shape)
    return lax.all_to_all(spread, axis, 0, 0, axis_index_groups=groups)


def all_conts(array):
    size = lax.axis_size("cont")
    side = math.isqrt(size)
    strided = [[k + side * j for j in range(side)] for k in range(side)]
    beside = [[side * j + k for k in range(side)] for j in range(side)]
    found = everyone(everyone(array, "cont", strided), "cont", beside)
    return jnp.swapaxes(found, 0, 1).reshape((size,) + array.shape)


def body(
    states,
    norm_gain,
    query_weight,
    key_weight,
    value_weight,
    prefix_keys,
    prefix_values,
    path_prefix,
    out_weight,
    final_gain,
    head_weight,
    targets,
    questions,
):
    path_count, path_length, width_block = states.shape
    head_width = prefix_keys.shape[-1]
    tensors, prefixes, conts = (lax.axis_size(a) for a in ("tensor", "prefix", "cont"))
    t, p, c = (lax.axis_index(a) for a in ("tensor", "prefix", "cont"))
    full_width = width_block * prefixes
    prefix_span = prefix_keys.shape[1] * conts
    positions = prefix_span + jnp.arange(path_length, dtype=jnp.int32)
    cosine, sine = rope_tables(head_width, positions)

    lead = jnp.concatenate([key_weight, value_weight, query_weight], 1)
    weights = lax.all_gather(lead, "cont", axis=0, tiled=True)
    gather_cache = lambda cache: lax.all_gather(
        cache.reshape(-1, head_width), "cont", axis=0, tiled=True
    )
    cached_keys, cached_values = gather_cache(prefix_keys), gather_cache(prefix_values)
    near_conts = conts // RESIDUES
    blocks_of = lambda size: [list(range(k, k + size)) for k in range(0, conts, size)]
    window = lax.all_gather(
        after(out_weight, weights),
        "cont",
        axis_index_groups=blocks_of(near_conts),
    )

    inputs = states.astype(jnp.float32)
    squares = jnp.sum(everyone(jnp.sum(inputs * inputs, axis=-1), "prefix"), axis=0)
    scaling = lax.rsqrt(squares / full_width + epsilon)
    normed = (inputs * scaling[..., None] * norm_gain).astype(jnp.bfloat16)
    normed = normed.reshape(path_count * path_length, width_block)

    def project(weight):
        full = jnp.dot(normed, weight, preferred_element_type=jnp.float32)
        return full.reshape(path_count, path_length, -1)

    owner_of = lambda q: lax.dynamic_index_in_dim(path_prefix, q, 0, keepdims=False)
    owner = owner_of(p)
    near = [(i, i ^ 1) for i in range(prefixes)]
    far = [(i, prefixes - 1 - i) for i in range(prefixes)]
    near_p, far_p = p ^ 1, prefixes - 1 - p

    middle = weights.shape[1] // 2
    left_part, right_part = project(weights[:, :middle]), project(weights[:, middle:])

    def choose(mine, first_perm, first_p, second_perm, second_p):
        beside = lax.ppermute(mine, "prefix", first_perm)
        sent = jnp.where(owner_of(second_p) == first_p, beside, mine)
        across = lax.ppermute(sent, "prefix", second_perm)
        across = after(across, left_part)
        return jnp.where(owner == p, mine, jnp.where(owner == first_p, beside, across))

    keys = choose(cached_keys, near, near_p, far, far_p)
    values = choose(cached_values, far, far_p, near, near_p)

    def path_sum(partial, first_perm, first_p, second_perm, second_p):
        pick = lambda q: lax.dynamic_index_in_dim(partial, q, 0, keepdims=False)
        third_p = p ^ first_p ^ second_p
        got = lax.ppermute(jnp.stack([pick(first_p), pick(third_p)]), "prefix", first_perm)
        passed = lax.ppermute(pick(second_p) + got[1], "prefix", second_perm)
        return pick(p) + got[0] + passed

    left = path_sum(left_part, near, near_p, far, far_p)
    right = path_sum(right_part, far, far_p, near, near_p)
    fresh_keys = rotate(left[:, :head_width], cosine, sine).astype(jnp.bfloat16)
    fresh_values = left[:, head_width : 2 * head_width].astype(jnp.bfloat16)
    queries = jnp.concatenate([left[:, 2 * head_width :], right], 1)
    context = attend(queries, cosine, sine, fresh_keys, fresh_values, keys, values)

    scored = context[path_length - SCORED :]
    share = [
        [q * conts + b + k * near_conts for q in range(prefixes) for k in range(RESIDUES)]
        for b in range(near_conts)
    ]
    rows = everyone(scored, ("prefix", "cont"), share)
    rows = rows.reshape(prefixes, RESIDUES, SCORED, -1).transpose(1, 0, 2, 3)
    scored_rows = rows.reshape(RESIDUES * path_count * SCORED, -1)
    cont_rows = path_count * SCORED
    sub_width = 2 * out_weight.shape[1]
    spans = tensors // RESIDUES
    pieces = pl.pallas_call(
        output_kernel,
        out_shape=jax.ShapeDtypeStruct((tensors, cont_rows, sub_width), jnp.float32),
        compiler_params=pltpu.CompilerParams(vmem_limit_bytes=24 * 1024 * 1024),
        cost_estimate=pl.CostEstimate(
            flops=2 * scored_rows.size * window.shape[0] * window.shape[2],
            bytes_accessed=2 * window.size,
            transcendentals=0,
        ),
    )(scored_rows, window)
    summed = jnp.sum(lax.all_to_all(pieces, "tensor", 0, 0), axis=0)
    perm = []
    for k in range(RESIDUES):
        for i in range(spans):
            for a in range(RESIDUES):
                for b in range(near_conts):
                    here = (k * spans + i) * conts + a * near_conts + b
                    perm.append((here, (a * spans + i) * conts + k * near_conts + b))
    summed = lax.ppermute(summed, ("tensor", "cont"), perm)

    residual = lax.dynamic_slice_in_dim(states[:, path_length - SCORED :, :], t * sub_width, sub_width, 2)
    hidden = (summed + residual.reshape(cont_rows, sub_width).astype(jnp.float32)).astype(jnp.bfloat16)

    every = all_conts(hidden).reshape(-1, sub_width).astype(jnp.float32)
    final_part = jnp.sum(every * every, axis=-1, keepdims=True)
    gained = (every * final_gain.reshape(sub_width)).astype(jnp.bfloat16)
    vocab_block = head_weight.shape[2]
    partial = jnp.dot(gained, head_weight.reshape(sub_width, vocab_block), preferred_element_type=jnp.float32)
    high = final_part.astype(jnp.bfloat16)
    low = (final_part - high.astype(jnp.float32)).astype(jnp.bfloat16)
    lanes = 128
    place = jnp.arange(lanes)[None, :]
    extra = jnp.where(place == 0, high, jnp.where(place == 1, low, jnp.zeros_like(high)))
    payload = jnp.concatenate([partial.astype(jnp.bfloat16), extra], 1)
    blocks = tensors * prefixes
    block_rows = targets.shape[0] * targets.shape[1]
    received = lax.all_to_all(
        payload.reshape(blocks, block_rows, vocab_block + lanes), ("tensor", "prefix"), 0, 0
    )
    received = jnp.sum(received.astype(jnp.float32), axis=0)
    final_sum = received[:, vocab_block] + received[:, vocab_block + 1]
    logits = received[:, :vocab_block] * lax.rsqrt(final_sum / full_width + epsilon)[:, None]

    wanted = targets.reshape(block_rows) - c * vocab_block
    matches = wanted[:, None] == jnp.arange(vocab_block, dtype=jnp.int32)[None, :]
    chosen = jnp.sum(jnp.where(matches, logits, 0.0), axis=-1)
    highest = jnp.max(logits, axis=-1)
    mass = jnp.sum(jnp.exp(logits - highest[:, None]), axis=-1)
    shares = all_conts(jnp.stack([highest, mass, chosen]))
    summit = jnp.max(shares[:, 0], axis=0)
    mass_all = jnp.sum(shares[:, 1] * jnp.exp(shares[:, 0] - summit), axis=0)
    token_logprob = (jnp.sum(shares[:, 2], axis=0) - (summit + jnp.log(mass_all))).reshape(targets.shape)
    path_score = jnp.mean(token_logprob, axis=-1)
    all_scores = everyone(path_score, ("tensor", "prefix")).reshape(-1)
    labels = jnp.arange(QUESTIONS, dtype=jnp.int32)
    member = (questions[:, 0][:, None] == labels[None, :]).astype(jnp.float32)
    question_score = jnp.sum(member * all_scores[:, None], axis=0) / jnp.sum(member, axis=0)
    return (
        context[None, None],
        hidden.reshape(path_count, SCORED, 1, sub_width),
        token_logprob,
        path_score,
        question_score,
    )


def solution(mesh):
    in_specs = (
        P("cont", None, "prefix"),
        P("prefix"),
        P(("prefix", "cont"), "tensor"),
        P(("prefix", "cont"), "tensor"),
        P(("prefix", "cont"), "tensor"),
        P("prefix", "cont", "tensor", None),
        P("prefix", "cont", "tensor", None),
        P("cont"),
        P("tensor", ("prefix", "cont")),
        P("prefix", "tensor"),
        P("prefix", "tensor", "cont"),
        P(("tensor", "prefix"), None),
        P(),
    )
    out_specs = (
        P("cont", "prefix", None, "tensor"),
        P("cont", None, "prefix", "tensor"),
        P(("tensor", "prefix"), None),
        P(("tensor", "prefix")),
        P(),
    )
    return jax.shard_map(body, mesh=mesh, in_specs=in_specs, out_specs=out_specs, check_vma=False)
```

```python
import math

import jax
import jax.numpy as jnp
from jax import lax
from jax.experimental import pallas as pl
from jax.experimental.pallas import tpu as pltpu
from jax.sharding import PartitionSpec as P

SCORED = 8
QUESTIONS = 8

epsilon = 1e-05
rope_base = 500000.0
far_below = -1e30


def rope_tables(head_width, positions):
    half_dim = head_width // 2
    ladder = jnp.arange(half_dim, dtype=jnp.float32) * (2.0 / head_width)
    inverse = jnp.exp(-math.log(rope_base) * ladder)
    angles = positions.astype(jnp.float32)[:, None] * inverse[None, :]
    cosine, sine = jnp.cos(angles), jnp.sin(angles)
    return jnp.concatenate([cosine, cosine], -1), jnp.concatenate([-sine, sine], -1)


def rotate(vectors, cosine, sine):
    half = vectors.shape[-1] // 2
    swapped = jnp.concatenate([vectors[..., half:], vectors[..., :half]], -1)
    return vectors * cosine + swapped * sine


def attend_kernel(q_ref, cos_ref, sin_ref, kf_ref, vf_ref, kp_ref, vp_ref, out_ref):
    length, width = cos_ref.shape
    heads = q_ref.shape[1] // width
    cosine, sine = cos_ref[...], sin_ref[...]
    turned = []
    for h in range(heads):
        q = q_ref[:, h * width : (h + 1) * width]
        turned.append((q * cosine + pltpu.roll(q, width // 2, 1) * sine).astype(jnp.bfloat16))
    queries = jnp.concatenate(turned, 0)
    contract = (((1,), (1,)), ((), ()))
    old = lax.dot_general(queries, kp_ref[...], contract, preferred_element_type=jnp.float32)
    new = lax.dot_general(queries, kf_ref[...], contract, preferred_element_type=jnp.float32)
    row = lax.broadcasted_iota(jnp.int32, (length, length), 0)
    column = lax.broadcasted_iota(jnp.int32, (length, length), 1)
    allowed = jnp.concatenate([column <= row] * heads, 0)
    new = jnp.where(allowed, new, far_below)
    peak = jnp.maximum(jnp.max(old, -1, keepdims=True), jnp.max(new, -1, keepdims=True))
    factor = math.log2(math.e) / math.sqrt(width)
    old = jnp.exp2((old - peak) * factor)
    new = jnp.exp2((new - peak) * factor)
    total = jnp.sum(old, -1, keepdims=True) + jnp.sum(new, -1, keepdims=True)
    mixed = jnp.dot(old.astype(jnp.bfloat16), vp_ref[...], preferred_element_type=jnp.float32)
    mixed += jnp.dot(new.astype(jnp.bfloat16), vf_ref[...], preferred_element_type=jnp.float32)
    mixed = (mixed / total).astype(jnp.bfloat16)
    for h in range(heads):
        out_ref[:, h * width : (h + 1) * width] = mixed[h * length : (h + 1) * length]


def attend(q, cosine, sine, fresh_keys, fresh_values, keys, values):
    length, columns = q.shape
    width = cosine.shape[1]
    pair = 2 * width
    whole = lambda array: pl.BlockSpec(array.shape, lambda i: (0, 0))
    count = (columns // width) * length * (keys.shape[0] + length)
    return pl.pallas_call(
        attend_kernel,
        grid=(columns // pair,),
        in_specs=[
            pl.BlockSpec((length, pair), lambda i: (0, i)),
            whole(cosine),
            whole(sine),
            whole(fresh_keys),
            whole(fresh_values),
            whole(keys),
            whole(values),
        ],
        out_specs=pl.BlockSpec((length, pair), lambda i: (0, i)),
        out_shape=jax.ShapeDtypeStruct((length, columns), jnp.bfloat16),
        compiler_params=pltpu.CompilerParams(vmem_limit_bytes=40 * 1024 * 1024),
        cost_estimate=pl.CostEstimate(
            flops=4 * count * width, bytes_accessed=2 * 1024 * 1024, transcendentals=count
        ),
    )(q, cosine, sine, fresh_keys, fresh_values, keys, values)


def after(array, earlier):
    return lax.optimization_barrier((array, earlier))[0]


def everyone(array, axis):
    size = lax.axis_size(axis)
    return lax.all_to_all(jnp.broadcast_to(array[None], (size,) + array.shape), axis, 0, 0)


def body(
    states,
    norm_gain,
    query_weight,
    key_weight,
    value_weight,
    prefix_keys,
    prefix_values,
    path_prefix,
    out_weight,
    final_gain,
    head_weight,
    targets,
    questions,
):
    path_count, path_length, width_block = states.shape
    head_width = prefix_keys.shape[-1]
    tensors, prefixes, conts = (lax.axis_size(a) for a in ("tensor", "prefix", "cont"))
    t, p, c = (lax.axis_index(a) for a in ("tensor", "prefix", "cont"))
    full_width = width_block * prefixes
    prefix_span = prefix_keys.shape[1] * conts
    positions = prefix_span + jnp.arange(path_length, dtype=jnp.int32)
    cosine, sine = rope_tables(head_width, positions)

    lead = jnp.concatenate([out_weight.T, key_weight, value_weight, query_weight], 1)
    gathered = lax.all_gather(lead, "cont", axis=0, tiled=True)
    depth = out_weight.shape[0]
    weights = gathered[:, depth:]
    gather_cache = lambda cache: lax.all_gather(
        cache.reshape(-1, head_width), "cont", axis=0, tiled=True
    )
    cached_keys, cached_values = gather_cache(prefix_keys), gather_cache(prefix_values)
    inputs = states.astype(jnp.float32)
    squares = jnp.sum(everyone(jnp.sum(inputs * inputs, axis=-1), "prefix"), axis=0)
    scaling = lax.rsqrt(squares / full_width + epsilon)
    normed = (inputs * scaling[..., None] * norm_gain).astype(jnp.bfloat16)
    normed = normed.reshape(path_count * path_length, width_block)

    def project(weight):
        full = jnp.dot(normed, weight, preferred_element_type=jnp.float32)
        return full.reshape(path_count, path_length, -1)

    owner_of = lambda q: lax.dynamic_index_in_dim(path_prefix, q, 0, keepdims=False)
    owner = owner_of(p)
    near = [(i, i ^ 1) for i in range(prefixes)]
    far = [(i, prefixes - 1 - i) for i in range(prefixes)]
    near_p, far_p = p ^ 1, prefixes - 1 - p

    middle = weights.shape[1] // 2
    left_part, right_part = project(weights[:, :middle]), project(weights[:, middle:])

    def choose(mine, first_perm, first_p, second_perm, second_p):
        beside = lax.ppermute(mine, "prefix", first_perm)
        sent = jnp.where(owner_of(second_p) == first_p, beside, mine)
        across = lax.ppermute(sent, "prefix", second_perm)
        across = after(across, left_part)
        return jnp.where(owner == p, mine, jnp.where(owner == first_p, beside, across))

    keys = choose(cached_keys, near, near_p, far, far_p)
    values = choose(cached_values, far, far_p, near, near_p)

    def path_sum(partial, first_perm, first_p, second_perm, second_p):
        pick = lambda q: lax.dynamic_index_in_dim(partial, q, 0, keepdims=False)
        third_p = p ^ first_p ^ second_p
        got = lax.ppermute(jnp.stack([pick(first_p), pick(third_p)]), "prefix", first_perm)
        passed = lax.ppermute(pick(second_p) + got[1], "prefix", second_perm)
        return pick(p) + got[0] + passed

    left = path_sum(left_part, near, near_p, far, far_p)
    right = path_sum(right_part, far, far_p, near, near_p)
    fresh_keys = rotate(left[:, :head_width], cosine, sine).astype(jnp.bfloat16)
    fresh_values = left[:, head_width : 2 * head_width].astype(jnp.bfloat16)
    queries = jnp.concatenate([left[:, 2 * head_width :], right], 1)
    context = attend(queries, cosine, sine, fresh_keys, fresh_values, keys, values)

    cont_rows = path_count * SCORED
    scored_rows = everyone(context[path_length - SCORED :], "prefix").reshape(cont_rows, -1)
    sub_width = 2 * out_weight.shape[1]
    projected = lax.dot_general(
        scored_rows,
        gathered[:, :depth],
        (((1,), (1,)), ((), ())),
        preferred_element_type=jnp.float32,
    )
    pieces = projected.reshape(cont_rows, tensors, sub_width).transpose(1, 0, 2)
    summed = jnp.sum(lax.all_to_all(pieces, "tensor", 0, 0), axis=0)
    residual = lax.dynamic_slice_in_dim(states[:, path_length - SCORED :, :], t * sub_width, sub_width, 2)
    hidden = (summed + residual.reshape(cont_rows, sub_width).astype(jnp.float32)).astype(jnp.bfloat16)

    every = lax.all_gather(hidden, "cont", axis=0, tiled=True).astype(jnp.float32)
    final_part = jnp.sum(every * every, axis=-1, keepdims=True)
    gained = (every * final_gain.reshape(sub_width)).astype(jnp.bfloat16)
    vocab_block = head_weight.shape[2]
    partial = jnp.dot(gained, head_weight.reshape(sub_width, vocab_block), preferred_element_type=jnp.float32)
    high = final_part.astype(jnp.bfloat16)
    low = (final_part - high.astype(jnp.float32)).astype(jnp.bfloat16)
    lanes = 128
    place = jnp.arange(lanes)[None, :]
    extra = jnp.where(place == 0, high, jnp.where(place == 1, low, jnp.zeros_like(high)))
    payload = jnp.concatenate([partial.astype(jnp.bfloat16), extra], 1)
    blocks = tensors * prefixes
    block_rows = targets.shape[0] * targets.shape[1]
    received = lax.all_to_all(
        payload.reshape(blocks, block_rows, vocab_block + lanes), ("tensor", "prefix"), 0, 0
    )
    received = jnp.sum(received.astype(jnp.float32), axis=0)
    final_sum = received[:, vocab_block] + received[:, vocab_block + 1]
    logits = received[:, :vocab_block] * lax.rsqrt(final_sum / full_width + epsilon)[:, None]

    wanted = targets.reshape(block_rows) - c * vocab_block
    matches = wanted[:, None] == jnp.arange(vocab_block, dtype=jnp.int32)[None, :]
    chosen = jnp.sum(jnp.where(matches, logits, 0.0), axis=-1)
    highest = jnp.max(logits, axis=-1)
    mass = jnp.sum(jnp.exp(logits - highest[:, None]), axis=-1)
    shares = everyone(jnp.stack([highest, mass, chosen]), "cont")
    summit = jnp.max(shares[:, 0], axis=0)
    mass_all = jnp.sum(shares[:, 1] * jnp.exp(shares[:, 0] - summit), axis=0)
    token_logprob = (jnp.sum(shares[:, 2], axis=0) - (summit + jnp.log(mass_all))).reshape(targets.shape)
    path_score = jnp.mean(token_logprob, axis=-1)
    all_scores = everyone(path_score, ("tensor", "prefix")).reshape(-1)
    labels = jnp.arange(QUESTIONS, dtype=jnp.int32)
    member = (questions[:, 0][:, None] == labels[None, :]).astype(jnp.float32)
    question_score = jnp.sum(member * all_scores[:, None], axis=0) / jnp.sum(member, axis=0)
    return (
        context[None, None],
        hidden.reshape(path_count, SCORED, 1, sub_width),
        token_logprob,
        path_score,
        question_score,
    )


def solution(mesh):
    in_specs = (
        P("cont", None, "prefix"),
        P("prefix"),
        P(("prefix", "cont"), "tensor"),
        P(("prefix", "cont"), "tensor"),
        P(("prefix", "cont"), "tensor"),
        P("prefix", "cont", "tensor", None),
        P("prefix", "cont", "tensor", None),
        P("cont"),
        P("tensor", ("prefix", "cont")),
        P("prefix", "tensor"),
        P("prefix", "tensor", "cont"),
        P(("tensor", "prefix"), None),
        P(),
    )
    out_specs = (
        P("cont", "prefix", None, "tensor"),
        P("cont", None, "prefix", "tensor"),
        P(("tensor", "prefix"), None),
        P(("tensor", "prefix")),
        P(),
    )
    return jax.shard_map(body, mesh=mesh, in_specs=in_specs, out_specs=out_specs, check_vma=False)
```

```python
import math

import jax
import jax.numpy as jnp
from jax import lax
from jax.experimental import pallas as pl
from jax.experimental.pallas import tpu as pltpu
from jax.sharding import PartitionSpec as P

SCORED = 8
QUESTIONS = 8

epsilon = 1e-05
rope_base = 500000.0
far_below = -1e30


def rope_tables(head_width, positions):
    half_dim = head_width // 2
    ladder = jnp.arange(half_dim, dtype=jnp.float32) * (2.0 / head_width)
    inverse = jnp.exp(-math.log(rope_base) * ladder)
    angles = positions.astype(jnp.float32)[:, None] * inverse[None, :]
    cosine, sine = jnp.cos(angles), jnp.sin(angles)
    return jnp.concatenate([cosine, cosine], -1), jnp.concatenate([-sine, sine], -1)


def rotate(vectors, cosine, sine):
    half = vectors.shape[-1] // 2
    swapped = jnp.concatenate([vectors[..., half:], vectors[..., :half]], -1)
    return vectors * cosine + swapped * sine


def attend_kernel(q_ref, cos_ref, sin_ref, kf_ref, vf_ref, kp_ref, vp_ref, out_ref):
    length, width = cos_ref.shape
    heads = q_ref.shape[1] // width
    cosine, sine = cos_ref[...], sin_ref[...]
    turned = []
    for h in range(heads):
        q = q_ref[:, h * width : (h + 1) * width]
        turned.append((q * cosine + pltpu.roll(q, width // 2, 1) * sine).astype(jnp.bfloat16))
    queries = jnp.concatenate(turned, 0)
    contract = (((1,), (1,)), ((), ()))
    old = lax.dot_general(queries, kp_ref[...], contract, preferred_element_type=jnp.float32)
    new = lax.dot_general(queries, kf_ref[...], contract, preferred_element_type=jnp.float32)
    row = lax.broadcasted_iota(jnp.int32, (length, length), 0)
    column = lax.broadcasted_iota(jnp.int32, (length, length), 1)
    allowed = jnp.concatenate([column <= row] * heads, 0)
    new = jnp.where(allowed, new, far_below)
    peak = jnp.maximum(jnp.max(old, -1, keepdims=True), jnp.max(new, -1, keepdims=True))
    factor = math.log2(math.e) / math.sqrt(width)
    old = jnp.exp2((old - peak) * factor)
    new = jnp.exp2((new - peak) * factor)
    total = jnp.sum(old, -1, keepdims=True) + jnp.sum(new, -1, keepdims=True)
    mixed = jnp.dot(old.astype(jnp.bfloat16), vp_ref[...], preferred_element_type=jnp.float32)
    mixed += jnp.dot(new.astype(jnp.bfloat16), vf_ref[...], preferred_element_type=jnp.float32)
    mixed = (mixed / total).astype(jnp.bfloat16)
    for h in range(heads):
        out_ref[:, h * width : (h + 1) * width] = mixed[h * length : (h + 1) * length]


def attend(q, cosine, sine, fresh_keys, fresh_values, keys, values):
    length, columns = q.shape
    width = cosine.shape[1]
    pair = 2 * width
    whole = lambda array: pl.BlockSpec(array.shape, lambda i: (0, 0))
    count = (columns // width) * length * (keys.shape[0] + length)
    return pl.pallas_call(
        attend_kernel,
        grid=(columns // pair,),
        in_specs=[
            pl.BlockSpec((length, pair), lambda i: (0, i)),
            whole(cosine),
            whole(sine),
            whole(fresh_keys),
            whole(fresh_values),
            whole(keys),
            whole(values),
        ],
        out_specs=pl.BlockSpec((length, pair), lambda i: (0, i)),
        out_shape=jax.ShapeDtypeStruct((length, columns), jnp.bfloat16),
        compiler_params=pltpu.CompilerParams(vmem_limit_bytes=40 * 1024 * 1024),
        cost_estimate=pl.CostEstimate(
            flops=4 * count * width, bytes_accessed=2 * 1024 * 1024, transcendentals=count
        ),
    )(q, cosine, sine, fresh_keys, fresh_values, keys, values)


def output_kernel(rows_ref, weight_ref, out_ref):
    blocks, _, width = weight_ref.shape
    rows = rows_ref[...]
    for j in range(blocks):
        out_ref[j // 2, :, (j % 2) * width : (j % 2 + 1) * width] = jnp.dot(
            rows, weight_ref[j], preferred_element_type=jnp.float32
        )


def after(array, earlier):
    return lax.optimization_barrier((array, earlier))[0]


def everyone(array, axis):
    size = lax.axis_size(axis)
    return lax.all_to_all(jnp.broadcast_to(array[None], (size,) + array.shape), axis, 0, 0)


def body(
    states,
    norm_gain,
    query_weight,
    key_weight,
    value_weight,
    prefix_keys,
    prefix_values,
    path_prefix,
    out_weight,
    final_gain,
    head_weight,
    targets,
    questions,
):
    path_count, path_length, width_block = states.shape
    head_width = prefix_keys.shape[-1]
    tensors, prefixes, conts = (lax.axis_size(a) for a in ("tensor", "prefix", "cont"))
    t, p, c = (lax.axis_index(a) for a in ("tensor", "prefix", "cont"))
    full_width = width_block * prefixes
    prefix_span = prefix_keys.shape[1] * conts
    positions = prefix_span + jnp.arange(path_length, dtype=jnp.int32)
    cosine, sine = rope_tables(head_width, positions)

    lead = jnp.concatenate([key_weight, value_weight, query_weight], 1)
    weights = lax.all_gather(lead, "cont", axis=0, tiled=True)
    gather_cache = lambda cache: lax.all_gather(
        cache.reshape(-1, head_width), "cont", axis=0, tiled=True
    )
    cached_keys, cached_values = gather_cache(prefix_keys), gather_cache(prefix_values)
    window = lax.all_gather(after(out_weight, (weights, cached_keys, cached_values)), "cont")

    inputs = states.astype(jnp.float32)
    squares = jnp.sum(everyone(jnp.sum(inputs * inputs, axis=-1), "prefix"), axis=0)
    scaling = lax.rsqrt(squares / full_width + epsilon)
    normed = (inputs * scaling[..., None] * norm_gain).astype(jnp.bfloat16)
    normed = normed.reshape(path_count * path_length, width_block)

    def project(weight):
        full = jnp.dot(normed, weight, preferred_element_type=jnp.float32)
        return full.reshape(path_count, path_length, -1)

    owner_of = lambda q: lax.dynamic_index_in_dim(path_prefix, q, 0, keepdims=False)
    owner = owner_of(p)
    near = [(i, i ^ 1) for i in range(prefixes)]
    far = [(i, prefixes - 1 - i) for i in range(prefixes)]
    near_p, far_p = p ^ 1, prefixes - 1 - p

    middle = weights.shape[1] // 2
    left_part, right_part = project(weights[:, :middle]), project(weights[:, middle:])

    def choose(mine, first_perm, first_p, second_perm, second_p):
        beside = lax.ppermute(mine, "prefix", first_perm)
        sent = jnp.where(owner_of(second_p) == first_p, beside, mine)
        across = lax.ppermute(sent, "prefix", second_perm)
        across = after(across, left_part)
        return jnp.where(owner == p, mine, jnp.where(owner == first_p, beside, across))

    keys = choose(cached_keys, near, near_p, far, far_p)
    values = choose(cached_values, far, far_p, near, near_p)

    def path_sum(partial, first_perm, first_p, second_perm, second_p):
        pick = lambda q: lax.dynamic_index_in_dim(partial, q, 0, keepdims=False)
        third_p = p ^ first_p ^ second_p
        got = lax.ppermute(jnp.stack([pick(first_p), pick(third_p)]), "prefix", first_perm)
        passed = lax.ppermute(pick(second_p) + got[1], "prefix", second_perm)
        return pick(p) + got[0] + passed

    left = path_sum(left_part, near, near_p, far, far_p)
    right = path_sum(right_part, far, far_p, near, near_p)
    fresh_keys = rotate(left[:, :head_width], cosine, sine).astype(jnp.bfloat16)
    fresh_values = left[:, head_width : 2 * head_width].astype(jnp.bfloat16)
    queries = jnp.concatenate([left[:, 2 * head_width :], right], 1)
    context = attend(queries, cosine, sine, fresh_keys, fresh_values, keys, values)

    cont_rows = path_count * SCORED
    scored_rows = everyone(context[path_length - SCORED :], "prefix").reshape(cont_rows, -1)
    sub_width = 2 * out_weight.shape[1]
    pieces = pl.pallas_call(
        output_kernel,
        out_shape=jax.ShapeDtypeStruct((tensors, cont_rows, sub_width), jnp.float32),
        compiler_params=pltpu.CompilerParams(vmem_limit_bytes=24 * 1024 * 1024),
        cost_estimate=pl.CostEstimate(
            flops=2 * scored_rows.size * window.shape[0] * window.shape[2],
            bytes_accessed=2 * window.size,
            transcendentals=0,
        ),
    )(scored_rows, window)
    summed = jnp.sum(lax.all_to_all(pieces, "tensor", 0, 0), axis=0)
    residual = lax.dynamic_slice_in_dim(states[:, path_length - SCORED :, :], t * sub_width, sub_width, 2)
    hidden = (summed + residual.reshape(cont_rows, sub_width).astype(jnp.float32)).astype(jnp.bfloat16)

    every = lax.all_gather(hidden, "cont", axis=0, tiled=True).astype(jnp.float32)
    final_part = jnp.sum(every * every, axis=-1, keepdims=True)
    gained = (every * final_gain.reshape(sub_width)).astype(jnp.bfloat16)
    vocab_block = head_weight.shape[2]
    partial = jnp.dot(gained, head_weight.reshape(sub_width, vocab_block), preferred_element_type=jnp.float32)
    high = final_part.astype(jnp.bfloat16)
    low = (final_part - high.astype(jnp.float32)).astype(jnp.bfloat16)
    lanes = 128
    place = jnp.arange(lanes)[None, :]
    extra = jnp.where(place == 0, high, jnp.where(place == 1, low, jnp.zeros_like(high)))
    payload = jnp.concatenate([partial.astype(jnp.bfloat16), extra], 1)
    blocks = tensors * prefixes
    block_rows = targets.shape[0] * targets.shape[1]
    received = lax.all_to_all(
        payload.reshape(blocks, block_rows, vocab_block + lanes), ("tensor", "prefix"), 0, 0
    )
    received = jnp.sum(received.astype(jnp.float32), axis=0)
    final_sum = received[:, vocab_block] + received[:, vocab_block + 1]
    logits = received[:, :vocab_block] * lax.rsqrt(final_sum / full_width + epsilon)[:, None]

    wanted = targets.reshape(block_rows) - c * vocab_block
    matches = wanted[:, None] == jnp.arange(vocab_block, dtype=jnp.int32)[None, :]
    chosen = jnp.sum(jnp.where(matches, logits, 0.0), axis=-1)
    highest = jnp.max(logits, axis=-1)
    mass = jnp.sum(jnp.exp(logits - highest[:, None]), axis=-1)
    shares = everyone(jnp.stack([highest, mass, chosen]), "cont")
    summit = jnp.max(shares[:, 0], axis=0)
    mass_all = jnp.sum(shares[:, 1] * jnp.exp(shares[:, 0] - summit), axis=0)
    token_logprob = (jnp.sum(shares[:, 2], axis=0) - (summit + jnp.log(mass_all))).reshape(targets.shape)
    path_score = jnp.mean(token_logprob, axis=-1)
    all_scores = everyone(path_score, ("tensor", "prefix")).reshape(-1)
    labels = jnp.arange(QUESTIONS, dtype=jnp.int32)
    member = (questions[:, 0][:, None] == labels[None, :]).astype(jnp.float32)
    question_score = jnp.sum(member * all_scores[:, None], axis=0) / jnp.sum(member, axis=0)
    return (
        context[None, None],
        hidden.reshape(path_count, SCORED, 1, sub_width),
        token_logprob,
        path_score,
        question_score,
    )


def solution(mesh):
    in_specs = (
        P("cont", None, "prefix"),
        P("prefix"),
        P(("prefix", "cont"), "tensor"),
        P(("prefix", "cont"), "tensor"),
        P(("prefix", "cont"), "tensor"),
        P("prefix", "cont", "tensor", None),
        P("prefix", "cont", "tensor", None),
        P("cont"),
        P("tensor", ("prefix", "cont")),
        P("prefix", "tensor"),
        P("prefix", "tensor", "cont"),
        P(("tensor", "prefix"), None),
        P(),
    )
    out_specs = (
        P("cont", "prefix", None, "tensor"),
        P("cont", None, "prefix", "tensor"),
        P(("tensor", "prefix"), None),
        P(("tensor", "prefix")),
        P(),
    )
    return jax.shard_map(body, mesh=mesh, in_specs=in_specs, out_specs=out_specs, check_vma=False)
```

```python
import math

import jax
import jax.numpy as jnp
from jax import lax
from jax.experimental import pallas as pl
from jax.experimental.pallas import tpu as pltpu
from jax.sharding import PartitionSpec as P

SCORED = 8
QUESTIONS = 8

epsilon = 1e-05
rope_base = 500000.0
far_below = -1e30


def rope_tables(head_width, positions):
    half_dim = head_width // 2
    ladder = jnp.arange(half_dim, dtype=jnp.float32) * (2.0 / head_width)
    inverse = jnp.exp(-math.log(rope_base) * ladder)
    angles = positions.astype(jnp.float32)[:, None] * inverse[None, :]
    cosine, sine = jnp.cos(angles), jnp.sin(angles)
    return jnp.concatenate([cosine, cosine], -1), jnp.concatenate([-sine, sine], -1)


def rotate(vectors, cosine, sine):
    half = vectors.shape[-1] // 2
    swapped = jnp.concatenate([vectors[..., half:], vectors[..., :half]], -1)
    return vectors * cosine + swapped * sine


def attend_kernel(q_ref, cos_ref, sin_ref, kf_ref, vf_ref, kp_ref, vp_ref, out_ref):
    length, width = cos_ref.shape
    fresh = kf_ref.shape[0]
    heads = q_ref.shape[1] // width
    cosine, sine = cos_ref[...], sin_ref[...]
    turned = []
    for h in range(heads):
        q = q_ref[:, h * width : (h + 1) * width]
        turned.append(q * cosine + pltpu.roll(q, width // 2, 1) * sine)
    queries = jnp.concatenate(turned, 0).astype(jnp.bfloat16)
    contract = (((1,), (1,)), ((), ()))
    old = lax.dot_general(queries, kp_ref[...], contract, preferred_element_type=jnp.float32)
    new = lax.dot_general(queries, kf_ref[...], contract, preferred_element_type=jnp.float32)
    row = lax.rem(lax.broadcasted_iota(jnp.int32, new.shape, 0), length) + (fresh - length)
    column = lax.broadcasted_iota(jnp.int32, new.shape, 1)
    new = jnp.where(column <= row, new, far_below)
    peak = jnp.maximum(jnp.max(old, -1, keepdims=True), jnp.max(new, -1, keepdims=True))
    factor = math.log2(math.e) / math.sqrt(width)
    old = jnp.exp2((old - peak) * factor)
    new = jnp.exp2((new - peak) * factor)
    total = jnp.sum(old, -1, keepdims=True) + jnp.sum(new, -1, keepdims=True)
    mixed = jnp.dot(old.astype(jnp.bfloat16), vp_ref[...], preferred_element_type=jnp.float32)
    mixed += jnp.dot(new.astype(jnp.bfloat16), vf_ref[...], preferred_element_type=jnp.float32)
    mixed = (mixed / total).astype(out_ref.dtype)
    for h in range(heads):
        out_ref[:, h * width : (h + 1) * width] = mixed[h * length : (h + 1) * length]


def attend(q, cosine, sine, fresh_keys, fresh_values, keys, values, heads, out_type):
    length, columns = q.shape
    width = cosine.shape[1]
    step = heads * width
    whole = lambda array: pl.BlockSpec(array.shape, lambda i: (0, 0))
    count = (columns // width) * length * (keys.shape[0] + fresh_keys.shape[0])
    return pl.pallas_call(
        attend_kernel,
        grid=(columns // step,),
        in_specs=[
            pl.BlockSpec((length, step), lambda i: (0, i)),
            whole(cosine),
            whole(sine),
            whole(fresh_keys),
            whole(fresh_values),
            whole(keys),
            whole(values),
        ],
        out_specs=pl.BlockSpec((length, step), lambda i: (0, i)),
        out_shape=jax.ShapeDtypeStruct((length, columns), out_type),
        compiler_params=pltpu.CompilerParams(vmem_limit_bytes=40 * 1024 * 1024),
        cost_estimate=pl.CostEstimate(
            flops=4 * count * width, bytes_accessed=2 * 1024 * 1024, transcendentals=count
        ),
    )(q, cosine, sine, fresh_keys, fresh_values, keys, values)


def after(array, earlier):
    return lax.optimization_barrier((array, earlier))[0]


def everyone(array, axis):
    size = lax.axis_size(axis)
    return lax.all_to_all(jnp.broadcast_to(array[None], (size,) + array.shape), axis, 0, 0)


def body(
    states,
    norm_gain,
    query_weight,
    key_weight,
    value_weight,
    prefix_keys,
    prefix_values,
    path_prefix,
    out_weight,
    final_gain,
    head_weight,
    targets,
    questions,
):
    path_count, path_length, width_block = states.shape
    head_width = prefix_keys.shape[-1]
    tensors, prefixes, conts = (lax.axis_size(a) for a in ("tensor", "prefix", "cont"))
    t, p, c = (lax.axis_index(a) for a in ("tensor", "prefix", "cont"))
    full_width = width_block * prefixes
    prefix_span = prefix_keys.shape[1] * conts
    positions = prefix_span + jnp.arange(path_length, dtype=jnp.int32)
    cosine, sine = rope_tables(head_width, positions)

    lead = jnp.concatenate([out_weight.T, key_weight, value_weight, query_weight], 1)
    gathered = lax.all_gather(lead, "cont", axis=0, tiled=True)
    depth = out_weight.shape[0]
    weights = gathered[:, depth:]
    gather_cache = lambda cache: lax.all_gather(
        cache.reshape(-1, head_width), "cont", axis=0, tiled=True
    )
    cached_keys, cached_values = gather_cache(prefix_keys), gather_cache(prefix_values)
    inputs = states.astype(jnp.float32)
    squares = jnp.sum(everyone(jnp.sum(inputs * inputs, axis=-1), "prefix"), axis=0)
    scaling = lax.rsqrt(squares / full_width + epsilon)
    normed = (inputs * scaling[..., None] * norm_gain).astype(jnp.bfloat16)
    normed = normed.reshape(path_count * path_length, width_block)

    def project(rows, weight):
        full = jnp.dot(rows, weight, preferred_element_type=jnp.float32)
        return full.reshape(path_count, -1, weight.shape[1])

    owner_of = lambda q: lax.dynamic_index_in_dim(path_prefix, q, 0, keepdims=False)
    owner = owner_of(p)
    near = [(i, i ^ 1) for i in range(prefixes)]
    far = [(i, prefixes - 1 - i) for i in range(prefixes)]
    near_p, far_p = p ^ 1, prefixes - 1 - p

    fresh_columns = 2 * head_width
    fresh_part = project(normed, weights[:, :fresh_columns])

    def choose(mine, first_perm, first_p, second_perm, second_p):
        beside = lax.ppermute(mine, "prefix", first_perm)
        sent = jnp.where(owner_of(second_p) == first_p, beside, mine)
        across = lax.ppermute(sent, "prefix", second_perm)
        across = after(across, fresh_part)
        return jnp.where(owner == p, mine, jnp.where(owner == first_p, beside, across))

    keys = choose(cached_keys, near, near_p, far, far_p)
    values = choose(cached_values, far, far_p, near, near_p)

    def path_sum(partial, first_perm, first_p, second_perm, second_p):
        pick = lambda q: lax.dynamic_index_in_dim(partial, q, 0, keepdims=False)
        third_p = p ^ first_p ^ second_p
        got = lax.ppermute(jnp.stack([pick(first_p), pick(third_p)]), "prefix", first_perm)
        passed = lax.ppermute(pick(second_p) + got[1], "prefix", second_perm)
        return pick(p) + got[0] + passed

    query_columns = weights.shape[1] - fresh_columns
    scored_normed = normed.reshape(path_count, path_length, -1)[:, path_length - SCORED :]
    scored_part = project(scored_normed.reshape(path_count * SCORED, -1), weights[:, fresh_columns:])
    scored_part = lax.optimization_barrier(scored_part)
    chunks = query_columns // fresh_columns
    scored_part = scored_part.reshape(path_count, SCORED, chunks, fresh_columns)
    scored_part = scored_part.transpose(0, 2, 1, 3).reshape(path_count, -1, fresh_columns)
    early = jnp.concatenate([fresh_part, scored_part], 1)
    early = jnp.sum(lax.all_to_all(early, "prefix", 0, 0), axis=0)
    fresh_keys = rotate(early[:path_length, :head_width], cosine, sine).astype(jnp.bfloat16)
    fresh_values = early[:path_length, head_width:].astype(jnp.bfloat16)
    scored_queries = early[path_length:].reshape(chunks, SCORED, fresh_columns)
    scored_queries = scored_queries.transpose(1, 0, 2).reshape(SCORED, query_columns)
    scored_context = attend(
        scored_queries,
        cosine[path_length - SCORED :],
        sine[path_length - SCORED :],
        fresh_keys,
        fresh_values,
        keys,
        values,
        query_columns // head_width,
        jnp.float32,
    ).astype(jnp.bfloat16)

    rows_later = after(normed, scored_context)
    middle = fresh_columns + query_columns // 2
    left = path_sum(project(rows_later, weights[:, fresh_columns:middle]), near, near_p, far, far_p)
    right = path_sum(project(rows_later, weights[:, middle:]), far, far_p, near, near_p)
    queries = jnp.concatenate([left, right], 1)

    cont_rows = path_count * SCORED
    scored_rows = everyone(scored_context, "prefix").reshape(cont_rows, -1)
    sub_width = 2 * out_weight.shape[1]
    projected = lax.dot_general(
        scored_rows,
        after(gathered, scored_context)[:, :depth],
        (((1,), (1,)), ((), ())),
        preferred_element_type=jnp.float32,
    )
    pieces = projected.reshape(cont_rows, tensors, sub_width).transpose(1, 0, 2)
    summed = jnp.sum(lax.all_to_all(pieces, "tensor", 0, 0), axis=0)
    residual = lax.dynamic_slice_in_dim(states[:, path_length - SCORED :, :], t * sub_width, sub_width, 2)
    hidden = (summed + residual.reshape(cont_rows, sub_width).astype(jnp.float32)).astype(jnp.bfloat16)

    every = lax.all_gather(hidden, "cont", axis=0, tiled=True).astype(jnp.float32)
    final_part = jnp.sum(every * every, axis=-1, keepdims=True)
    gained = (every * final_gain.reshape(sub_width)).astype(jnp.bfloat16)
    vocab_block = head_weight.shape[2]
    partial = jnp.dot(gained, head_weight.reshape(sub_width, vocab_block), preferred_element_type=jnp.float32)
    high = final_part.astype(jnp.bfloat16)
    low = (final_part - high.astype(jnp.float32)).astype(jnp.bfloat16)
    lanes = 128
    place = jnp.arange(lanes)[None, :]
    extra = jnp.where(place == 0, high, jnp.where(place == 1, low, jnp.zeros_like(high)))
    payload = jnp.concatenate([partial.astype(jnp.bfloat16), extra], 1)
    blocks = tensors * prefixes
    block_rows = targets.shape[0] * targets.shape[1]
    context = attend(
        after(queries, payload),
        cosine,
        sine,
        fresh_keys,
        fresh_values,
        keys,
        values,
        2,
        jnp.bfloat16,
    )
    received = lax.all_to_all(
        payload.reshape(blocks, block_rows, vocab_block + lanes), ("tensor", "prefix"), 0, 0
    )
    received = jnp.sum(after(received, context).astype(jnp.float32), axis=0)
    final_sum = received[:, vocab_block] + received[:, vocab_block + 1]
    logits = received[:, :vocab_block] * lax.rsqrt(final_sum / full_width + epsilon)[:, None]

    wanted = targets.reshape(block_rows) - c * vocab_block
    matches = wanted[:, None] == jnp.arange(vocab_block, dtype=jnp.int32)[None, :]
    chosen = jnp.sum(jnp.where(matches, logits, 0.0), axis=-1)
    highest = jnp.max(logits, axis=-1)
    mass = jnp.sum(jnp.exp(logits - highest[:, None]), axis=-1)
    shares = everyone(jnp.stack([highest, mass, chosen]), "cont")
    summit = jnp.max(shares[:, 0], axis=0)
    mass_all = jnp.sum(shares[:, 1] * jnp.exp(shares[:, 0] - summit), axis=0)
    token_logprob = (jnp.sum(shares[:, 2], axis=0) - (summit + jnp.log(mass_all))).reshape(targets.shape)
    path_score = jnp.mean(token_logprob, axis=-1)
    all_scores = everyone(path_score, ("tensor", "prefix")).reshape(-1)
    labels = jnp.arange(QUESTIONS, dtype=jnp.int32)
    member = (questions[:, 0][:, None] == labels[None, :]).astype(jnp.float32)
    question_score = jnp.sum(member * all_scores[:, None], axis=0) / jnp.sum(member, axis=0)
    return (
        context[None, None],
        hidden.reshape(path_count, SCORED, 1, sub_width),
        token_logprob,
        path_score,
        question_score,
    )


def solution(mesh):
    in_specs = (
        P("cont", None, "prefix"),
        P("prefix"),
        P(("prefix", "cont"), "tensor"),
        P(("prefix", "cont"), "tensor"),
        P(("prefix", "cont"), "tensor"),
        P("prefix", "cont", "tensor", None),
        P("prefix", "cont", "tensor", None),
        P("cont"),
        P("tensor", ("prefix", "cont")),
        P("prefix", "tensor"),
        P("prefix", "tensor", "cont"),
        P(("tensor", "prefix"), None),
        P(),
    )
    out_specs = (
        P("cont", "prefix", None, "tensor"),
        P("cont", None, "prefix", "tensor"),
        P(("tensor", "prefix"), None),
        P(("tensor", "prefix")),
        P(),
    )
    return jax.shard_map(body, mesh=mesh, in_specs=in_specs, out_specs=out_specs, check_vma=False)
```

```python
import math

import jax
import jax.numpy as jnp
from jax import lax
from jax.experimental import pallas as pl
from jax.experimental.pallas import tpu as pltpu
from jax.sharding import PartitionSpec as P

SCORED = 8
QUESTIONS = 8

epsilon = 1e-05
rope_base = 500000.0
far_below = -1e30


def rope_tables(head_width, positions):
    half_dim = head_width // 2
    ladder = jnp.arange(half_dim, dtype=jnp.float32) * (2.0 / head_width)
    inverse = jnp.exp(-math.log(rope_base) * ladder)
    angles = positions.astype(jnp.float32)[:, None] * inverse[None, :]
    cosine, sine = jnp.cos(angles), jnp.sin(angles)
    return jnp.concatenate([cosine, cosine], -1), jnp.concatenate([-sine, sine], -1)


def rotate(vectors, cosine, sine):
    half = vectors.shape[-1] // 2
    swapped = jnp.concatenate([vectors[..., half:], vectors[..., :half]], -1)
    return vectors * cosine + swapped * sine


def attend_kernel(q_ref, cos_ref, sin_ref, kf_ref, vf_ref, kp_ref, vp_ref, out_ref):
    length, width = cos_ref.shape
    heads = q_ref.shape[1] // width
    cosine, sine = cos_ref[...], sin_ref[...]
    turned = []
    for h in range(heads):
        q = q_ref[:, h * width : (h + 1) * width]
        turned.append((q * cosine + pltpu.roll(q, width // 2, 1) * sine).astype(jnp.bfloat16))
    queries = jnp.concatenate(turned, 0)
    contract = (((1,), (1,)), ((), ()))
    old = lax.dot_general(queries, kp_ref[...], contract, preferred_element_type=jnp.float32)
    new = lax.dot_general(queries, kf_ref[...], contract, preferred_element_type=jnp.float32)
    row = lax.broadcasted_iota(jnp.int32, (length, length), 0)
    column = lax.broadcasted_iota(jnp.int32, (length, length), 1)
    allowed = jnp.concatenate([column <= row] * heads, 0)
    new = jnp.where(allowed, new, far_below)
    peak = jnp.maximum(jnp.max(old, -1, keepdims=True), jnp.max(new, -1, keepdims=True))
    factor = math.log2(math.e) / math.sqrt(width)
    old = jnp.exp2((old - peak) * factor)
    new = jnp.exp2((new - peak) * factor)
    total = jnp.sum(old, -1, keepdims=True) + jnp.sum(new, -1, keepdims=True)
    mixed = jnp.dot(old.astype(jnp.bfloat16), vp_ref[...], preferred_element_type=jnp.float32)
    mixed += jnp.dot(new.astype(jnp.bfloat16), vf_ref[...], preferred_element_type=jnp.float32)
    mixed = (mixed / total).astype(jnp.bfloat16)
    for h in range(heads):
        out_ref[:, h * width : (h + 1) * width] = mixed[h * length : (h + 1) * length]


def attend(q, cosine, sine, fresh_keys, fresh_values, keys, values):
    length, columns = q.shape
    width = cosine.shape[1]
    pair = 2 * width
    whole = lambda array: pl.BlockSpec(array.shape, lambda i: (0, 0))
    count = (columns // width) * length * (keys.shape[0] + length)
    return pl.pallas_call(
        attend_kernel,
        grid=(columns // pair,),
        in_specs=[
            pl.BlockSpec((length, pair), lambda i: (0, i)),
            whole(cosine),
            whole(sine),
            whole(fresh_keys),
            whole(fresh_values),
            whole(keys),
            whole(values),
        ],
        out_specs=pl.BlockSpec((length, pair), lambda i: (0, i)),
        out_shape=jax.ShapeDtypeStruct((length, columns), jnp.bfloat16),
        compiler_params=pltpu.CompilerParams(vmem_limit_bytes=40 * 1024 * 1024),
        cost_estimate=pl.CostEstimate(
            flops=4 * count * width, bytes_accessed=2 * 1024 * 1024, transcendentals=count
        ),
    )(q, cosine, sine, fresh_keys, fresh_values, keys, values)


def output_kernel(rows_ref, weight_ref, out_ref):
    blocks, _, width = weight_ref.shape
    rows = rows_ref[...]
    for j in range(blocks):
        out_ref[0, :, j * width : (j + 1) * width] = jnp.dot(
            rows, weight_ref[j], preferred_element_type=jnp.float32
        )


def after(array, earlier):
    return lax.optimization_barrier((array, earlier))[0]


def everyone(array, axis):
    size = lax.axis_size(axis)
    return lax.all_to_all(jnp.broadcast_to(array[None], (size,) + array.shape), axis, 0, 0)


def body(
    states,
    norm_gain,
    query_weight,
    key_weight,
    value_weight,
    prefix_keys,
    prefix_values,
    path_prefix,
    out_weight,
    final_gain,
    head_weight,
    targets,
    questions,
):
    path_count, path_length, width_block = states.shape
    head_width = prefix_keys.shape[-1]
    tensors, prefixes, conts = (lax.axis_size(a) for a in ("tensor", "prefix", "cont"))
    t, p, c = (lax.axis_index(a) for a in ("tensor", "prefix", "cont"))
    full_width = width_block * prefixes
    prefix_span = prefix_keys.shape[1] * conts
    positions = prefix_span + jnp.arange(path_length, dtype=jnp.int32)
    cosine, sine = rope_tables(head_width, positions)

    lead = jnp.concatenate([key_weight, value_weight, query_weight], 1)
    weights = lax.all_gather(lead, "cont", axis=0, tiled=True)
    gather_cache = lambda cache: lax.all_gather(
        cache.reshape(-1, head_width), "cont", axis=0, tiled=True
    )
    cached_keys, cached_values = gather_cache(prefix_keys), gather_cache(prefix_values)
    window = lax.all_gather(after(out_weight, (cached_keys, cached_values)), "cont")

    inputs = states.astype(jnp.float32)
    squares = jnp.sum(everyone(jnp.sum(inputs * inputs, axis=-1), "prefix"), axis=0)
    scaling = lax.rsqrt(squares / full_width + epsilon)
    normed = (inputs * scaling[..., None] * norm_gain).astype(jnp.bfloat16)
    normed = normed.reshape(path_count * path_length, width_block)

    def project(weight):
        full = jnp.dot(normed, weight, preferred_element_type=jnp.float32)
        return full.reshape(path_count, path_length, -1)

    owner_of = lambda q: lax.dynamic_index_in_dim(path_prefix, q, 0, keepdims=False)
    owner = owner_of(p)
    near = [(i, i ^ 1) for i in range(prefixes)]
    far = [(i, prefixes - 1 - i) for i in range(prefixes)]
    near_p, far_p = p ^ 1, prefixes - 1 - p

    middle = weights.shape[1] // 2
    left_part, right_part = project(weights[:, :middle]), project(weights[:, middle:])

    def choose(mine, first_perm, first_p, second_perm, second_p):
        beside = lax.ppermute(mine, "prefix", first_perm)
        sent = jnp.where(owner_of(second_p) == first_p, beside, mine)
        across = lax.ppermute(sent, "prefix", second_perm)
        across = after(across, left_part)
        return jnp.where(owner == p, mine, jnp.where(owner == first_p, beside, across))

    keys = choose(cached_keys, near, near_p, far, far_p)
    values = choose(cached_values, far, far_p, near, near_p)

    def path_sum(partial, first_perm, first_p, second_perm, second_p):
        pick = lambda q: lax.dynamic_index_in_dim(partial, q, 0, keepdims=False)
        third_p = p ^ first_p ^ second_p
        got = lax.ppermute(jnp.stack([pick(first_p), pick(third_p)]), "prefix", first_perm)
        passed = lax.ppermute(pick(second_p) + got[1], "prefix", second_perm)
        return pick(p) + got[0] + passed

    left = path_sum(left_part, near, near_p, far, far_p)
    right = path_sum(right_part, far, far_p, near, near_p)
    fresh_keys = rotate(left[:, :head_width], cosine, sine).astype(jnp.bfloat16)
    fresh_values = left[:, head_width : 2 * head_width].astype(jnp.bfloat16)
    queries = jnp.concatenate([left[:, 2 * head_width :], right], 1)
    context = attend(queries, cosine, sine, fresh_keys, fresh_values, keys, values)

    cont_rows = path_count * SCORED
    scored_rows = everyone(context[path_length - SCORED :], "prefix").reshape(cont_rows, -1)
    sub_width = 2 * out_weight.shape[1]
    depth, width = out_weight.shape
    pieces = pl.pallas_call(
        output_kernel,
        grid=(tensors,),
        in_specs=[
            pl.BlockSpec(scored_rows.shape, lambda i: (0, 0)),
            pl.BlockSpec((2, depth, width), lambda i: (i, 0, 0)),
        ],
        out_specs=pl.BlockSpec((1, cont_rows, sub_width), lambda i: (i, 0, 0)),
        out_shape=jax.ShapeDtypeStruct((tensors, cont_rows, sub_width), jnp.float32),
        compiler_params=pltpu.CompilerParams(vmem_limit_bytes=56 * 1024 * 1024),
        cost_estimate=pl.CostEstimate(
            flops=2 * cont_rows * window.size, bytes_accessed=2 * window.size, transcendentals=0
        ),
    )(scored_rows, window)
    summed = jnp.sum(lax.all_to_all(pieces, "tensor", 0, 0), axis=0)
    residual = lax.dynamic_slice_in_dim(states[:, path_length - SCORED :, :], t * sub_width, sub_width, 2)
    hidden = (summed + residual.reshape(cont_rows, sub_width).astype(jnp.float32)).astype(jnp.bfloat16)

    every = lax.all_gather(hidden, "cont", axis=0, tiled=True).astype(jnp.float32)
    final_part = jnp.sum(every * every, axis=-1, keepdims=True)
    gained = (every * final_gain.reshape(sub_width)).astype(jnp.bfloat16)
    vocab_block = head_weight.shape[2]
    partial = jnp.dot(gained, head_weight.reshape(sub_width, vocab_block), preferred_element_type=jnp.float32)
    high = final_part.astype(jnp.bfloat16)
    low = (final_part - high.astype(jnp.float32)).astype(jnp.bfloat16)
    lanes = 128
    place = jnp.arange(lanes)[None, :]
    extra = jnp.where(place == 0, high, jnp.where(place == 1, low, jnp.zeros_like(high)))
    payload = jnp.concatenate([partial.astype(jnp.bfloat16), extra], 1)
    blocks = tensors * prefixes
    block_rows = targets.shape[0] * targets.shape[1]
    received = lax.all_to_all(
        payload.reshape(blocks, block_rows, vocab_block + lanes), ("tensor", "prefix"), 0, 0
    )
    received = jnp.sum(received.astype(jnp.float32), axis=0)
    final_sum = received[:, vocab_block] + received[:, vocab_block + 1]
    logits = received[:, :vocab_block] * lax.rsqrt(final_sum / full_width + epsilon)[:, None]

    wanted = targets.reshape(block_rows) - c * vocab_block
    matches = wanted[:, None] == jnp.arange(vocab_block, dtype=jnp.int32)[None, :]
    chosen = jnp.sum(jnp.where(matches, logits, 0.0), axis=-1)
    highest = jnp.max(logits, axis=-1)
    mass = jnp.sum(jnp.exp(logits - highest[:, None]), axis=-1)
    shares = everyone(jnp.stack([highest, mass, chosen]), "cont")
    summit = jnp.max(shares[:, 0], axis=0)
    mass_all = jnp.sum(shares[:, 1] * jnp.exp(shares[:, 0] - summit), axis=0)
    token_logprob = (jnp.sum(shares[:, 2], axis=0) - (summit + jnp.log(mass_all))).reshape(targets.shape)
    path_score = jnp.mean(token_logprob, axis=-1)
    labels = jnp.arange(QUESTIONS, dtype=jnp.int32)
    member = (questions[:, 0][None, :] == labels[:, None]).astype(jnp.float32)
    share = (member / jnp.sum(member, axis=1, keepdims=True)).reshape(QUESTIONS, blocks, -1)
    all_scores = everyone(path_score, ("tensor", "prefix"))
    question_score = jnp.sum(share * all_scores.reshape(blocks, -1), axis=(1, 2))
    return (
        context[None, None],
        hidden.reshape(path_count, SCORED, 1, sub_width),
        token_logprob,
        path_score,
        question_score,
    )


def solution(mesh):
    in_specs = (
        P("cont", None, "prefix"),
        P("prefix"),
        P(("prefix", "cont"), "tensor"),
        P(("prefix", "cont"), "tensor"),
        P(("prefix", "cont"), "tensor"),
        P("prefix", "cont", "tensor", None),
        P("prefix", "cont", "tensor", None),
        P("cont"),
        P("tensor", ("prefix", "cont")),
        P("prefix", "tensor"),
        P("prefix", "tensor", "cont"),
        P(("tensor", "prefix"), None),
        P(),
    )
    out_specs = (
        P("cont", "prefix", None, "tensor"),
        P("cont", None, "prefix", "tensor"),
        P(("tensor", "prefix"), None),
        P(("tensor", "prefix")),
        P(),
    )
    return jax.shard_map(body, mesh=mesh, in_specs=in_specs, out_specs=out_specs, check_vma=False)
```
